128 devices in a mesh: tgt: 8 (over y, core), src: 16 (over z, x).
Axes of the slice: x: 4, y: 4, z: 4, core: 2. Of those that a mesh axis runs over, the one named last changes fastest.
Arguments:
- mobility: bfloat16 [3, 3, 8, 16, 64, 8192], P(None, None, None, 'src', None, 'tgt'), may hold values from -0.0390625 to 0.0390625
- right_side: float32 [3, 8192, 512], P(None, ('tgt', 'src')), may hold values from -6 to 6
- precond: float32 [96, 24576], P(None, ('tgt', 'src')), may hold values from -0.5 to 2.5
Outputs:
- solution: float32 [3, 8192, 512], P(None, ('tgt', 'src'))
- arnoldi: float32 [3, 2, 512], replicated
The draws below stay inside these ranges and needn't reach their ends.
All inputs are finite; a program needn't handle non-finite values.
Results may differ from the reference program's by a relative error of at most 0.0012.
Values may be sent and summed in bfloat16 or wider, within the bound.
A program may use at most 64 MiB of HBM per device.

```python
import jax
import jax.numpy as jnp
from jax import lax

FIBER_NODES = 32
CASES = 512
NODE_DEV = 64
NODES = 8192
N_TGT = 8
N_SRC = 16


def draw_precond(key, part):
    fibers = NODES // FIBER_NODES
    width = 3 * FIBER_NODES
    key_one, key_two = jax.random.split(jax.random.fold_in(key, 23), 2)
    diagonal = jnp.exp(jax.random.uniform(key_one, (fibers, width), jnp.float32, jnp.log(0.5), jnp.log(2.0)))
    spread = jnp.clip(jax.random.normal(key_two, (fibers, width, width), jnp.float32), -6.0, 6.0) * (0.4 / jnp.sqrt(float(width)))
    blocks = spread + diagonal[:, :, None] * jnp.eye(width, dtype=jnp.float32)[None]
    return blocks.transpose(1, 0, 2).reshape(width, fibers * width).astype(jnp.float32)


def shard_levels(key, dims, cuts, least, high):
    factor_of = 1.0
    for dim, blocks in cuts:
        heights = jax.random.uniform(jax.random.fold_in(jax.random.fold_in(key, 6), dim), (blocks,), jnp.float32, least / len(cuts), high / len(cuts))
        factor_of = factor_of * jnp.repeat(jnp.exp(heights), dims[dim] // blocks).reshape((-1,) + (1,) * (len(dims) - 1 - dim))
    return factor_of


def noise(rng, dims, scale, limit, cuts=(), held_as=jnp.bfloat16):
    values = jax.random.normal(rng, dims, jnp.float32) * scale
    if len(cuts) > 0:
        values = shard_levels(rng, dims, cuts, -0.22, 0.18) * values
    return jnp.clip(values, min=-limit, max=limit).astype(held_as)


def setup_inputs(seed: int = 0) -> dict:
    keys = jax.random.split(jax.random.key(seed), 4)
    mobility = noise(keys[0], (3, 3, N_TGT, N_SRC, NODE_DEV, NODES), (3 * NODES) ** -0.5, 0.0390625, ((3, 16), (5, 8)))
    right_side = noise(keys[1], (3, NODES, CASES), 1.0, 6.0, ((1, 128),), jnp.float32)
    precond = draw_precond(jax.random.fold_in(keys[3], 71), 0)
    return dict(mobility=mobility, right_side=right_side, precond=precond)


def couple(mobility, vector):
    matrix = mobility.reshape(3, 3, NODES, NODES)
    rounded = vector.astype(jnp.bfloat16)
    parts = []
    for comp in range(3):
        total = jnp.zeros((NODES, vector.shape[2]), jnp.float32)
        for source in range(3):
            total = total + lax.dot_general(matrix[source, comp], rounded[source], (((0,), (0,)), ((), ())), preferred_element_type=jnp.float32)
        parts.append(total)
    return jnp.stack(parts)

def apply_blocks(blocks, vector):
    width = 3 * FIBER_NODES
    fibers = blocks.shape[1] // width
    case_count = vector.shape[2]
    tiles = blocks.reshape(width, fibers, width)
    arranged = vector.reshape(3, fibers, FIBER_NODES, case_count).transpose(1, 0, 2, 3).reshape(fibers, width, case_count)
    result = jnp.einsum('afb,fbr->far', tiles, arranged, precision=lax.Precision.HIGHEST)
    return result.reshape(fibers, 3, FIBER_NODES, case_count).transpose(1, 0, 2, 3).reshape(3, fibers * FIBER_NODES, case_count)

def least_squares(beta, h_one_one, h_two_one, h_one_two, h_two_two, h_three_two):
    rho_one = jnp.sqrt(h_one_one * h_one_one + h_two_one * h_two_one)
    cos_one = h_one_one / rho_one
    sin_one = h_two_one / rho_one
    g_one = cos_one * beta
    g_two = -sin_one * beta
    top = cos_one * h_one_two + sin_one * h_two_two
    low = cos_one * h_two_two - sin_one * h_one_two
    rho_two = jnp.sqrt(low * low + h_three_two * h_three_two)
    cos_two = low / rho_two
    sin_two = h_three_two / rho_two
    y_two = cos_two * g_two / rho_two
    y_one = (g_one - top * y_two) / rho_one
    return (y_one, y_two, jnp.abs(sin_two * g_two))

def inner(first, second):
    return lax.optimization_barrier(jnp.sum(first * second, axis=(0, 1)))

def reference(mobility, right_side, precond):

    def operate(vector):
        return vector + couple(mobility, vector)
    initial = apply_blocks(precond, right_side)
    beta = jnp.sqrt(inner(initial, initial) + 1e-06)
    basis_one = initial / beta[None, None, :]
    work = apply_blocks(precond, operate(basis_one))
    h_one_one = inner(basis_one, work)
    work = work - h_one_one[None, None, :] * basis_one
    h_two_one = jnp.sqrt(inner(work, work) + 1e-06)
    basis_two = work / h_two_one[None, None, :]
    other = apply_blocks(precond, operate(basis_two))
    h_one_two = inner(basis_one, other)
    h_two_two = inner(basis_two, other)
    other = other - h_one_two[None, None, :] * basis_one - h_two_two[None, None, :] * basis_two
    h_three_two = jnp.sqrt(inner(other, other) + 1e-06)
    y_one, y_two, estimate = least_squares(beta, h_one_one, h_two_one, h_one_two, h_two_two, h_three_two)
    solution = y_one[None, None, :] * basis_one + y_two[None, None, :] * basis_two
    arnoldi = jnp.stack([jnp.stack([h_one_one, h_one_two]), jnp.stack([h_two_one, h_two_two]), jnp.stack([estimate, h_three_two])])
    return (solution, arnoldi)
```

```python
import jax
import jax.numpy as jnp
from jax import lax
from jax.experimental import pallas as pl
from jax.experimental.pallas import tpu as pltpu
from jax.sharding import PartitionSpec as P

MESH = pl.DeviceIdType.MESH
F32 = jnp.float32
BF16 = jnp.bfloat16
HIGHEST = lax.Precision.HIGHEST
LANES = 256
EPS = 1e-06


def least_squares(beta, h_one_one, h_two_one, h_one_two, h_two_two, h_three_two):
    rho_one = jnp.sqrt(h_one_one * h_one_one + h_two_one * h_two_one)
    cos_one = h_one_one / rho_one
    sin_one = h_two_one / rho_one
    g_one = cos_one * beta
    g_two = -sin_one * beta
    top = cos_one * h_one_two + sin_one * h_two_two
    low = cos_one * h_two_two - sin_one * h_one_two
    rho_two = jnp.sqrt(low * low + h_three_two * h_three_two)
    cos_two = low / rho_two
    sin_two = h_three_two / rho_two
    y_two = cos_two * g_two / rho_two
    y_one = (g_one - top * y_two) / rho_one
    return (y_one, y_two, jnp.abs(sin_two * g_two))


def kernel(
    mob, rhs, pre, sol, arn,
    stage, mt, v1, w, o, q1, snd1, rcv1, snd2, rcv2, g, ar1, ar2,
    mob_sem, rs_send, rs_recv, g_send, g_recv, ar_send, ar_recv,
):
    t = lax.axis_index("tgt")
    s = lax.axis_index("src")
    y, core = t // 2, t % 2
    z, x = s // 4, s % 4
    pos = {"z": z, "x": x}

    def at(p, k):
        return (p + k + 4) % 4

    loads = [pltpu.make_async_copy(mob.at[j], stage.at[j], mob_sem.at[j]) for j in range(9)]
    for load in loads:
        load.start()
    barrier = pltpu.get_barrier_semaphore()

    def greet_src(k, carry):
        pl.semaphore_signal(barrier, inc=1, device_id=(t, (s + k) % 16), device_id_type=MESH)
        return carry

    def greet_tgt(k, carry):
        pl.semaphore_signal(barrier, inc=1, device_id=((t + k) % 8, s), device_id_type=MESH)
        return carry

    lax.fori_loop(1, 16, greet_src, 0)
    lax.fori_loop(1, 8, greet_tgt, 0)

    def apply_blocks(first, second):
        zeros = jnp.zeros_like(first)
        both = jnp.concatenate(
            [jnp.concatenate([first, zeros], axis=0), jnp.concatenate([zeros, second], axis=0)], axis=1
        )
        out = jnp.dot(pre[...], both, precision=HIGHEST, preferred_element_type=F32)
        n = first.shape[1]
        return out[:, :n], out[:, n:]

    def inner(a, b):
        return jnp.sum(a[0] * b[0], axis=0, keepdims=True) + jnp.sum(a[1] * b[1], axis=0, keepdims=True)

    def ar_tile(rows):
        parts = [r[:, j * 128:(j + 1) * 128] for r in rows for j in range(r.shape[1] // 128)]
        parts = parts + [jnp.zeros((1, 128), F32)] * (8 - len(parts))
        return jnp.concatenate(parts, axis=0)

    def ar_copy1(i, slot, target):
        return pltpu.make_async_remote_copy(
            src_ref=ar1.at[i, slot], dst_ref=ar1.at[i, slot], send_sem=ar_send.at[i, 0],
            recv_sem=ar_recv.at[i, 0], device_id=(t, target), device_id_type=MESH)

    def ar_copy2(i, slot, target):
        return pltpu.make_async_remote_copy(
            src_ref=ar2.at[i, slot], dst_ref=ar2.at[i, slot], send_sem=ar_send.at[i, 1],
            recv_sem=ar_recv.at[i, 1], device_id=(target, s), device_id_type=MESH)

    def ar_all1(i):
        return ar_copy1(i, pl.ds(0, 15), at_src(1))

    def ar_all2(i):
        return ar_copy2(i, pl.ds(0, 7), (t + 1) % 8)

    def at_src(k):
        return (s + k) % 16

    def ar_start(i, rows):
        ar1[i, s] = ar_tile(rows)

        def send(k, carry):
            ar_copy1(i, s, (s + k) % 16).start()
            return carry

        lax.fori_loop(1, 16, send, 0)

    def ar_mid(i):
        ar_all1(i).wait_recv()
        total = ar1[i, 0]
        for k in range(1, 16):
            total = total + ar1[i, k]
        ar2[i, t] = total

        def send(k, carry):
            ar_copy2(i, t, (t + k) % 8).start()
            return carry

        lax.fori_loop(1, 8, send, 0)

    def ar_end(i):
        ar_all2(i).wait_recv()
        total = ar2[i, 0]
        for k in range(1, 8):
            total = total + ar2[i, k]
        return total

    def row(tile, first, count):
        return jnp.concatenate([tile[first + j:first + j + 1] for j in range(count)], axis=1)

    def piece(k, c):
        return at(y, k) * 2 + c

    def g_ref(op, b, which, half):
        if half is None:
            return g.at[op, b, :, which]
        return g.at[op, b, :, which, pl.ds(half * 32, 32)]

    other = 1 - core
    sib = (y * 2 + other, s)
    up = (piece(1, core), s)
    down = (piece(-1, core), s)
    routes = [
        (t, piece(0, other), None, sib),
        (t, piece(-1, core), None, up),
        (t, piece(1, core), None, down),
        (piece(-1, core), piece(2, core), 0, up),
        (piece(-1, core), piece(-1, other), None, sib),
        (piece(1, core), piece(2, core), 1, down),
        (piece(1, core), piece(1, other), None, sib),
        (piece(2, core), piece(2, other), 0, sib),
        (piece(2, core), piece(2, other), 1, sib),
    ]

    def g_copy(op, b, i, sent):
        out, into, half, target = routes[i]
        ref = g_ref(op, b, out if sent else into, half)
        return pltpu.make_async_remote_copy(
            src_ref=ref, dst_ref=ref, send_sem=g_send.at[op, b, i], recv_sem=g_recv.at[op, b, i],
            device_id=target, device_id_type=MESH)

    def g_start(op, b, vec):
        for f in range(2):
            for c in range(3):
                g[op, b, c, t, f * 32:(f + 1) * 32, :] = vec[f][c * 32:(c + 1) * 32].astype(BF16)
        for i in (1, 2, 0):
            g_copy(op, b, i, True).start()

    def g_forward(op, b):
        g_copy(op, b, 1, False).wait_recv()
        g_copy(op, b, 3, True).start()
        g_copy(op, b, 4, True).start()
        g_copy(op, b, 2, False).wait_recv()
        g_copy(op, b, 5, True).start()
        g_copy(op, b, 6, True).start()

    def g_last(op, b):
        g_copy(op, b, 3, False).wait_recv()
        g_copy(op, b, 7, True).start()
        g_copy(op, b, 5, False).wait_recv()
        g_copy(op, b, 8, True).start()

    def g_finish(op, b):
        for i in (0, 4, 6, 7, 8):
            g_copy(op, b, i, False).wait_recv()

    def multiply(op, b):
        def block(i, carry):
            c, zz = i // 4, i % 4
            rows = mt[c, pl.ds(pl.multiple_of(zz * 256, 256), 256), :]
            acc = jnp.dot(rows, g[op, b].reshape(1536, LANES), preferred_element_type=F32)
            acc = acc.reshape(4, 64, LANES)
            o[b, 0, c, zz] = acc[:, :, :128]
            o[b, 1, c, zz] = acc[:, :, 128:]
            return carry

        lax.fori_loop(0, 12, block, 0)

    rings = (("z", "x"), ("x", "z"))

    def neighbour(ring, d):
        k = 1 - 2 * d
        if ring == "z":
            return (t, at(z, k) * 4 + x)
        return (t, z * 4 + at(x, k))

    def rs_copy(op, b, fl, st, m):
        snd, rcv = (snd1, rcv1) if st == 0 else (snd2, rcv2)
        return pltpu.make_async_remote_copy(
            src_ref=snd.at[op, b, fl, m], dst_ref=rcv.at[op, b, fl, m],
            send_sem=rs_send.at[op, b, fl, st, m], recv_sem=rs_recv.at[op, b, fl, st, m],
            device_id=neighbour(rings[fl][st], m // 3), device_id_type=MESH)

    def own(b, fl, st, k, half):
        grp = at(pos[rings[fl][st]], k)
        if st == 1:
            return q1[b, fl, :, grp, half * 32:half * 32 + 32]
        if fl == 0:
            return o[b, 0, :, grp, half * 2:half * 2 + 2]
        return o[b, 1, :, half * 2:half * 2 + 2, grp]

    def rs_first(op, b, st, kind):
        snd = (snd1, snd2)[st]
        for fl in range(2):
            for d in range(2):
                m = d * 3 + kind
                if kind == 0:
                    val = own(b, fl, st, 2, d)
                else:
                    val = own(b, fl, st, 1 - 2 * d, 1 - d)
                snd[op, b, fl, m] = val.astype(BF16)
                rs_copy(op, b, fl, st, m).start()

    def rs_forward(op, b, st):
        snd, rcv = (snd1, rcv1) if st == 0 else (snd2, rcv2)
        for fl in range(2):
            for d in range(2):
                rs_copy(op, b, fl, st, d * 3).wait_recv()
                val = own(b, fl, st, 1 - 2 * d, d) + rcv[op, b, fl, d * 3].astype(F32)
                snd[op, b, fl, d * 3 + 2] = val.astype(BF16)
                rs_copy(op, b, fl, st, d * 3 + 2).start()

    def rs_sum(op, b, fl, st):
        rcv = (rcv1, rcv2)[st]
        for m in (1, 4, 2, 5):
            rs_copy(op, b, fl, st, m).wait_recv()
        return [
            own(b, fl, st, 0, half) + rcv[op, b, fl, 2 - half].astype(F32) + rcv[op, b, fl, 4 + half].astype(F32)
            for half in range(2)
        ]

    def rs_middle(op, b):
        for fl in range(2):
            halves = rs_sum(op, b, fl, 0)
            for half in range(2):
                q1[b, fl, :, half * 2:half * 2 + 2] = halves[half]

    def rs_end(op, b):
        parts = [rs_sum(op, b, fl, 1) for fl in range(2)]
        return [
            jnp.concatenate([parts[fl][f].reshape(96, 128) for fl in range(2)], axis=1) for f in range(2)
        ]

    def cols(b):
        return slice(b * LANES, (b + 1) * LANES)

    def get(ref, b):
        return [ref[f, :, cols(b)] for f in range(2)]

    def fiber(f):
        return jnp.concatenate([rhs[c, f * 32:(f + 1) * 32, :] for c in range(3)], axis=0)

    r0 = apply_blocks(fiber(0), fiber(1))
    for f in range(2):
        v1[f] = r0[f]
    pl.semaphore_wait(barrier, 22)
    ar_start(0, [inner(r0, r0)])

    eye = (
        lax.broadcasted_iota(jnp.int32, (256, 256), 0) == lax.broadcasted_iota(jnp.int32, (256, 256), 1)
    ).astype(F32).astype(BF16)

    def turn(j):
        loads[j].wait()
        c2, c = j // 3, j % 3

        def block(i, carry):
            cut = pl.ds(pl.multiple_of(i * 256, 256), 256)
            for kb in range(2):
                tile = stage[j, kb * 256:(kb + 1) * 256, cut]
                turned = lax.dot_general(eye, tile, (((1,), (1,)), ((), ())), preferred_element_type=F32)
                mt[c, cut, c2 * 512 + kb * 256:c2 * 512 + (kb + 1) * 256] = turned.astype(BF16)
            return carry

        lax.fori_loop(0, 4, block, 0)

    for j in range(3):
        turn(j)
    ar_mid(0)
    for j in range(3, 5):
        turn(j)
    square = row(ar_end(0), 0, 4)
    beta_all = jnp.sqrt(square + EPS)
    for f in range(2):
        v1[f] = v1[f] / beta_all
    g_start(0, 0, get(v1, 0))
    g_start(0, 1, get(v1, 1))
    for j in range(5, 7):
        turn(j)
    g_forward(0, 0)
    turn(7)
    g_forward(0, 1)
    turn(8)
    g_last(0, 0)
    g_last(0, 1)
    g_finish(0, 0)

    betas = [beta_all[:, cols(b)] for b in range(2)]
    squares = [square[:, cols(b)] for b in range(2)]
    h11, h21, n22 = [None, None], [None, None], [None, None]

    def after_first(b):
        kv = rs_end(0, b)
        vec = get(v1, b)
        wv = apply_blocks(vec[0] + kv[0], vec[1] + kv[1])
        for f in range(2):
            w[f, :, cols(b)] = wv[f]
        g_start(1, b, wv)
        ar_start(1 + b, [inner(vec, wv), inner(wv, wv)])

    def second_basis(b):
        tile = ar_end(1 + b)
        h = row(tile, 0, 2)
        ww = row(tile, 2, 2)
        n11 = squares[b] / (squares[b] + EPS)
        left = jnp.maximum(ww - h * h * (2.0 - n11), 0.0)
        h11[b] = h
        h21[b] = jnp.sqrt(left + EPS)
        n22[b] = left / (left + EPS)

    def after_second(b):
        kw = rs_end(1, b)
        first, wv = get(v1, b), get(w, b)
        q = apply_blocks(wv[0] + kw[0], wv[1] + kw[1])
        second = [(wv[f] - h11[b] * first[f]) / h21[b] for f in range(2)]
        zv = [(q[f] - h11[b] * wv[f]) / h21[b] for f in range(2)]
        ar_start(3 + b, [inner(first, zv), inner(second, zv), inner(zv, zv)])
        for f in range(2):
            w[f, :, cols(b)] = second[f]

    def output(b):
        tile = ar_end(3 + b)
        h12, h22, zz = row(tile, 0, 2), row(tile, 2, 2), row(tile, 4, 2)
        n11 = squares[b] / (squares[b] + EPS)
        n12 = h11[b] * (1.0 - n11) / h21[b]
        left = zz - h12 * h12 * (2.0 - n11) - h22 * h22 * (2.0 - n22[b]) + 2.0 * h12 * h22 * n12
        h32 = jnp.sqrt(jnp.maximum(left, 0.0) + EPS)
        y1, y2, estimate = least_squares(betas[b], h11[b], h21[b], h12, h22, h32)
        for f in range(2):
            out = y1 * v1[f, :, cols(b)] + y2 * w[f, :, cols(b)]
            for c in range(3):
                sol[c, f * 32:(f + 1) * 32, cols(b)] = out[c * 32:(c + 1) * 32]
        for i, pair in enumerate(((h11[b], h12), (h21[b], h22), (estimate, h32))):
            for j in range(2):
                arn[i, j:j + 1, cols(b)] = pair[j]

    multiply(0, 0)
    rs_first(0, 0, 0, 0)
    rs_first(0, 0, 0, 1)
    g_finish(0, 1)
    multiply(0, 1)
    rs_forward(0, 0, 0)
    rs_first(0, 1, 0, 0)
    rs_middle(0, 0)
    rs_first(0, 0, 1, 0)
    rs_first(0, 0, 1, 1)
    rs_first(0, 1, 0, 1)
    rs_forward(0, 0, 1)
    rs_forward(0, 1, 0)
    after_first(0)
    rs_middle(0, 1)
    rs_first(0, 1, 1, 0)
    rs_first(0, 1, 1, 1)
    g_forward(1, 0)
    rs_forward(0, 1, 1)
    ar_mid(1)
    g_last(1, 0)
    g_finish(1, 0)
    multiply(1, 0)
    rs_first(1, 0, 0, 0)
    rs_first(1, 0, 0, 1)
    after_first(1)
    g_forward(1, 1)
    second_basis(0)
    rs_forward(1, 0, 0)
    g_last(1, 1)
    ar_mid(2)
    g_finish(1, 1)
    multiply(1, 1)
    rs_first(1, 1, 0, 0)
    rs_middle(1, 0)
    rs_first(1, 0, 1, 0)
    rs_first(1, 0, 1, 1)
    rs_first(1, 1, 0, 1)
    second_basis(1)
    rs_forward(1, 0, 1)
    rs_forward(1, 1, 0)
    after_second(0)
    rs_middle(1, 1)
    rs_first(1, 1, 1, 0)
    rs_first(1, 1, 1, 1)
    ar_mid(3)
    rs_forward(1, 1, 1)
    after_second(1)
    output(0)
    ar_mid(4)
    output(1)

    for op in range(2):
        for b in range(2):
            for fl in range(2):
                for st in range(2):
                    for m in range(6):
                        rs_copy(op, b, fl, st, m).wait_send()
            for i in range(9):
                g_copy(op, b, i, True).wait_send()
    for i in range(5):
        ar_all1(i).wait_send()
        ar_all2(i).wait_send()


def local(mobility, right_side, precond):
    mob = mobility.reshape(9, 512, 1024)
    vmem = pl.BlockSpec(memory_space=pltpu.VMEM)
    dma = pltpu.SemaphoreType.DMA
    return pl.pallas_call(
        kernel,
        out_shape=(jax.ShapeDtypeStruct((3, 64, 512), F32), jax.ShapeDtypeStruct((3, 2, 512), F32)),
        in_specs=[pl.BlockSpec(memory_space=pl.ANY), vmem, vmem],
        out_specs=(vmem, vmem),
        scratch_shapes=[
            pltpu.VMEM((9, 512, 1024), BF16),
            pltpu.VMEM((3, 1024, 1536), BF16),
            pltpu.VMEM((2, 96, 512), F32),
            pltpu.VMEM((2, 96, 512), F32),
            pltpu.VMEM((2, 2, 3, 4, 4, 64, 128), F32),
            pltpu.VMEM((2, 2, 3, 4, 64, 128), F32),
            pltpu.VMEM((2, 2, 2, 6, 3, 2, 64, 128), BF16),
            pltpu.VMEM((2, 2, 2, 6, 3, 2, 64, 128), BF16),
            pltpu.VMEM((2, 2, 2, 6, 3, 32, 128), BF16),
            pltpu.VMEM((2, 2, 2, 6, 3, 32, 128), BF16),
            pltpu.VMEM((2, 2, 3, 8, 64, LANES), BF16),
            pltpu.VMEM((5, 16, 8, 128), F32),
            pltpu.VMEM((5, 8, 8, 128), F32),
            dma((9,)),
            dma((2, 2, 2, 2, 6)),
            dma((2, 2, 2, 2, 6)),
            dma((2, 2, 9)),
            dma((2, 2, 9)),
            dma((5, 2)),
            dma((5, 2)),
        ],
        compiler_params=pltpu.CompilerParams(
            collective_id=0, has_side_effects=True, vmem_limit_bytes=60 * 1024 * 1024
        ),
    )(mob, right_side, precond)


def solution(mesh):
    return jax.shard_map(
        local,
        mesh=mesh,
        in_specs=(P(None, None, None, "src", None, "tgt"), P(None, ("tgt", "src"), None), P(None, ("tgt", "src"))),
        out_specs=(P(None, ("tgt", "src"), None), P()),
        check_vma=False,
    )
```

```python
import jax
import jax.numpy as jnp
from jax import lax
from jax.experimental import pallas as pl
from jax.experimental.pallas import tpu as pltpu
from jax.sharding import PartitionSpec as P

MESH = pl.DeviceIdType.MESH
F32 = jnp.float32
BF16 = jnp.bfloat16
HIGHEST = lax.Precision.HIGHEST
LANES = 128
EPS = 1e-06


def least_squares(beta, h_one_one, h_two_one, h_one_two, h_two_two, h_three_two):
    rho_one = jnp.sqrt(h_one_one * h_one_one + h_two_one * h_two_one)
    cos_one = h_one_one / rho_one
    sin_one = h_two_one / rho_one
    g_one = cos_one * beta
    g_two = -sin_one * beta
    top = cos_one * h_one_two + sin_one * h_two_two
    low = cos_one * h_two_two - sin_one * h_one_two
    rho_two = jnp.sqrt(low * low + h_three_two * h_three_two)
    cos_two = low / rho_two
    sin_two = h_three_two / rho_two
    y_two = cos_two * g_two / rho_two
    y_one = (g_one - top * y_two) / rho_one
    return (y_one, y_two, jnp.abs(sin_two * g_two))


BATCHES = 4


def kernel(
    mob, rhs, pre, sol, arn,
    stage, mt, v1, w, o, q1, snd1, rcv1, snd2, rcv2, wide, g, ar1, ar2,
    mob_sem, rs_send, rs_recv, g_send, g_recv, ar_send, ar_recv,
):
    t = lax.axis_index("tgt")
    s = lax.axis_index("src")
    y, core = t // 2, t % 2
    z, x = s // 4, s % 4
    pos = {"z": z, "x": x}

    def at(p, k):
        return (p + k + 4) % 4

    sent, due = {}, {}

    def begin(key, out, into):
        out.start()
        sent[key], due[key] = out, into

    def arrived(key):
        due.pop(key).wait_recv()

    loads = [pltpu.make_async_copy(mob.at[j], stage.at[j], mob_sem.at[j]) for j in range(9)]
    for load in loads:
        load.start()
    barrier = pltpu.get_barrier_semaphore()
    for k in range(1, 16):
        pl.semaphore_signal(barrier, inc=1, device_id=(t, (s + k) % 16), device_id_type=MESH)
    for k in range(1, 8):
        pl.semaphore_signal(barrier, inc=1, device_id=((t + k) % 8, s), device_id_type=MESH)

    def apply_blocks(first, second):
        zeros = jnp.zeros_like(first)
        both = jnp.concatenate(
            [jnp.concatenate([first, zeros], axis=0), jnp.concatenate([zeros, second], axis=0)], axis=1
        )
        out = jnp.dot(pre[...], both, precision=HIGHEST, preferred_element_type=F32)
        n = first.shape[1]
        return out[:, :n], out[:, n:]

    def inner(a, b):
        return jnp.sum(a[0] * b[0], axis=0, keepdims=True) + jnp.sum(a[1] * b[1], axis=0, keepdims=True)

    def ar_copy1(i, slot, target):
        return pltpu.make_async_remote_copy(
            src_ref=ar1.at[i, slot], dst_ref=ar1.at[i, slot], send_sem=ar_send.at[i, 0],
            recv_sem=ar_recv.at[i, 0], device_id=(t, target), device_id_type=MESH)

    def ar_copy2(i, slot, target):
        return pltpu.make_async_remote_copy(
            src_ref=ar2.at[i, slot], dst_ref=ar2.at[i, slot], send_sem=ar_send.at[i, 1],
            recv_sem=ar_recv.at[i, 1], device_id=(target, s), device_id_type=MESH)

    def ar_start(i, rows):
        ar1[i, s] = jnp.concatenate(rows + [jnp.zeros((8 - len(rows), 128), F32)], axis=0)
        for k in range(1, 16):
            ar_copy1(i, s, (s + k) % 16).start()
        sent["a", i] = due["a", i] = ar_copy1(i, pl.ds(0, 15), (s + 1) % 16)

    def ar_mid(i):
        arrived(("a", i))
        total = ar1[i, 0]
        for k in range(1, 16):
            total = total + ar1[i, k]
        ar2[i, t] = total
        for k in range(1, 8):
            ar_copy2(i, t, (t + k) % 8).start()
        sent["b", i] = due["b", i] = ar_copy2(i, pl.ds(0, 7), (t + 1) % 8)

    def ar_end(i):
        arrived(("b", i))
        total = ar2[i, 0]
        for k in range(1, 8):
            total = total + ar2[i, k]
        return [total[k:k + 1] for k in range(8)]

    other = 1 - core
    sib = (y * 2 + other, s)

    def g_copy(op, b, i, out):
        ref = wide.at[b] if op == 0 else g.at[op, b]
        if i == 0:
            part, target = (t if out else y * 2 + other), sib
        elif i < 4:
            part, target = (t if out else at(y, -i) * 2 + core), (at(y, i) * 2 + core, s)
        else:
            part, target = at(y, 3 - i) * 2 + (core if out else other), sib
        return pltpu.make_async_remote_copy(
            src_ref=ref.at[:, part], dst_ref=ref.at[:, part], send_sem=g_send.at[op, b, i],
            recv_sem=g_recv.at[op, b, i], device_id=target, device_id_type=MESH)

    def g_send_one(op, b, i):
        begin(("g", op, b, i), g_copy(op, b, i, True), g_copy(op, b, i, False))

    def g_start(op, b, vec):
        for f in range(2):
            for c in range(3):
                val = vec[f][c * 32:(c + 1) * 32]
                if op == 0:
                    wide[b, c, t, f * 32:(f + 1) * 32, :] = val
                else:
                    g[op, b, c, t, f * 32:(f + 1) * 32, :] = val.astype(BF16)
        for i in (2, 1, 3, 0):
            g_send_one(op, b, i)

    def g_forward(op, b):
        for i in (1, 3, 2):
            arrived(("g", op, b, i))
            g_send_one(op, b, i + 3)

    def g_finish(op, b):
        for i in (0, 4, 6, 5):
            arrived(("g", op, b, i))

    def multiply(op, b):
        def block(i, carry):
            c, zz = i // 4, i % 4
            rows = mt[c, pl.ds(pl.multiple_of(zz * 256, 256), 256), :]
            acc = jnp.dot(rows, g[op, b].reshape(1536, LANES), preferred_element_type=F32)
            o[b, c, zz] = acc.reshape(4, 64, LANES)
            return carry

        lax.fori_loop(0, 12, block, 0)

    order = (("z", "x"), ("x", "z"))

    def device(ring, k):
        if ring == "z":
            return (t, at(z, k) * 4 + x)
        return (t, z * 4 + at(x, k))

    def rs_send_one(op, b, fl, m, val):
        if m < 6:
            snd, rcv = snd1.at[op, b, fl, m], rcv1.at[op, b, fl, m]
            target = device(order[fl][0], 1 - 2 * (m // 3))
        else:
            snd, rcv = snd2.at[op, b, fl, m - 6], rcv2.at[op, b, fl, m - 6]
            target = device(order[fl][1], m - 5)
        snd[...] = val.astype(BF16)
        copy = pltpu.make_async_remote_copy(
            src_ref=snd, dst_ref=rcv, send_sem=rs_send.at[op, b, fl, m], recv_sem=rs_recv.at[op, b, fl, m],
            device_id=target, device_id_type=MESH)
        begin(("r", op, b, fl, m), copy, copy)

    def own(b, fl, k, half):
        grp = at(pos[order[fl][0]], k)
        if fl == 0:
            return o[b, :, grp, half * 2:half * 2 + 2, 0:32]
        return o[b, :, half * 2:half * 2 + 2, grp, 32:64]

    def rs_first(op, b):
        for d in range(2):
            for fl in range(2):
                rs_send_one(op, b, fl, d * 3, own(b, fl, 2, d))
        for d in range(2):
            for fl in range(2):
                rs_send_one(op, b, fl, d * 3 + 1, own(b, fl, 1 - 2 * d, 1 - d))

    def rs_forward(op, b):
        for d in range(2):
            for fl in range(2):
                arrived(("r", op, b, fl, d * 3))
                rs_send_one(op, b, fl, d * 3 + 2, own(b, fl, 1 - 2 * d, d) + rcv1[op, b, fl, d * 3].astype(F32))

    def rs_middle(op, b):
        for fl in range(2):
            for m in (1, 4, 2, 5):
                arrived(("r", op, b, fl, m))
            for half in range(2):
                q1[b, fl, :, half * 2:half * 2 + 2] = (
                    own(b, fl, 0, half) + rcv1[op, b, fl, 2 - half].astype(F32) + rcv1[op, b, fl, 4 + half].astype(F32)
                )
            for k in (2, 1, 3):
                rs_send_one(op, b, fl, 5 + k, q1[b, fl, :, at(pos[order[fl][1]], k)])

    def rs_end(op, b):
        out = []
        for fl in range(2):
            total = q1[b, fl, :, pos[order[fl][1]]]
            for k in (1, 3, 2):
                arrived(("r", op, b, fl, 5 + k))
                total = total + rcv2[op, b, fl, k - 1].astype(F32)
            out.append(total.reshape(96, LANES))
        return out

    def cols(b):
        return slice(b * LANES, (b + 1) * LANES)

    def get(ref, b):
        return [ref[f, :, cols(b)] for f in range(2)]

    eye = (
        lax.broadcasted_iota(jnp.int32, (256, 256), 0) == lax.broadcasted_iota(jnp.int32, (256, 256), 1)
    ).astype(F32).astype(BF16)

    def turn(j):
        loads[j].wait()
        c2, c = j // 3, j % 3

        def block(i, carry):
            cut = pl.ds(pl.multiple_of(i * 256, 256), 256)
            for kb in range(2):
                tile = stage[j, kb * 256:(kb + 1) * 256, cut]
                turned = lax.dot_general(eye, tile, (((1,), (1,)), ((), ())), preferred_element_type=F32)
                mt[c, cut, c2 * 512 + kb * 256:c2 * 512 + (kb + 1) * 256] = turned.astype(BF16)
            return carry

        lax.fori_loop(0, 4, block, 0)

    def fiber(f):
        return jnp.concatenate([rhs[c, f * 32:(f + 1) * 32, :] for c in range(3)], axis=0)

    def start():
        r0 = apply_blocks(fiber(0), fiber(1))
        for f in range(2):
            v1[f] = r0[f]

    def greeted():
        pl.semaphore_wait(barrier, 22)
        ar_start(0, [inner(get(v1, b), get(v1, b)) for b in range(BATCHES)])
        for b in range(BATCHES):
            g_start(0, b, get(v1, b))

    betas, squares = [None] * BATCHES, [None] * BATCHES
    h11, h21, n22 = [None] * BATCHES, [None] * BATCHES, [None] * BATCHES
    kept = {}

    def first_basis():
        tile = ar_end(0)
        for b in range(BATCHES):
            squares[b] = tile[b]
            betas[b] = jnp.sqrt(tile[b] + EPS)
            for f in range(2):
                v1[f, :, cols(b)] = v1[f, :, cols(b)] / betas[b]

    def normalise(b):
        g_finish(0, b)
        for c in range(3):
            g[0, b, c] = (wide[b, c] / betas[b].reshape(1, 1, LANES)).astype(BF16)

    def after_first(b):
        kv = rs_end(0, b)
        vec = get(v1, b)
        wv = apply_blocks(vec[0] + kv[0], vec[1] + kv[1])
        for f in range(2):
            w[f, :, cols(b)] = wv[f]
        g_start(1, b, wv)
        kept[b] = [inner(vec, wv), inner(wv, wv)]
        if b % 2 == 1:
            ar_start(1 + b // 2, kept[b - 1] + kept[b])

    def second_basis(pair):
        tile = ar_end(1 + pair)
        for j in range(2):
            b = pair * 2 + j
            h, ww = tile[j * 2], tile[j * 2 + 1]
            n11 = squares[b] / (squares[b] + EPS)
            left = jnp.maximum(ww - h * h * (2.0 - n11), 0.0)
            h11[b] = h
            h21[b] = jnp.sqrt(left + EPS)
            n22[b] = left / (left + EPS)

    def after_second(b):
        kw = rs_end(1, b)
        first, wv = get(v1, b), get(w, b)
        q = apply_blocks(wv[0] + kw[0], wv[1] + kw[1])
        second = [(wv[f] - h11[b] * first[f]) / h21[b] for f in range(2)]
        zv = [(q[f] - h11[b] * wv[f]) / h21[b] for f in range(2)]
        for f in range(2):
            w[f, :, cols(b)] = second[f]
        kept[b] = [inner(first, zv), inner(second, zv), inner(zv, zv)]
        if b % 2 == 1:
            ar_start(3 + b // 2, kept[b - 1] + kept[b])

    def output(pair):
        tile = ar_end(3 + pair)
        for j in range(2):
            b = pair * 2 + j
            h12, h22, zz = tile[j * 3:j * 3 + 3]
            n11 = squares[b] / (squares[b] + EPS)
            n12 = h11[b] * (1.0 - n11) / h21[b]
            left = zz - h12 * h12 * (2.0 - n11) - h22 * h22 * (2.0 - n22[b]) + 2.0 * h12 * h22 * n12
            h32 = jnp.sqrt(jnp.maximum(left, 0.0) + EPS)
            y1, y2, estimate = least_squares(betas[b], h11[b], h21[b], h12, h22, h32)
            for f in range(2):
                out = y1 * v1[f, :, cols(b)] + y2 * w[f, :, cols(b)]
                for c in range(3):
                    sol[c, f * 32:(f + 1) * 32, cols(b)] = out[c * 32:(c + 1) * 32]
            for i, row in enumerate(((h11[b], h12), (h21[b], h22), (estimate, h32))):
                for k in range(2):
                    arn[i, k:k + 1, cols(b)] = row[k]

    def spread(op, b):
        if op == 0:
            normalise(b)
        else:
            g_finish(1, b)
        multiply(op, b)
        rs_first(op, b)

    steps = [
        (start,), (turn, 0), (turn, 1), (turn, 2), (turn, 3), (greeted,),
        (turn, 4), (turn, 5), (turn, 6), (turn, 7), (turn, 8), (ar_mid, 0), (g_forward, 0, 0), (first_basis,),
        (spread, 0, 0), (g_forward, 0, 1), (rs_forward, 0, 0),
        (spread, 0, 1), (g_forward, 0, 2), (rs_middle, 0, 0), (rs_forward, 0, 1),
        (spread, 0, 2), (g_forward, 0, 3), (rs_middle, 0, 1), (after_first, 0), (rs_forward, 0, 2),
        (spread, 0, 3), (rs_middle, 0, 2), (after_first, 1), (rs_forward, 0, 3), (g_forward, 1, 0),
        (spread, 1, 0), (ar_mid, 1), (rs_middle, 0, 3), (after_first, 2), (g_forward, 1, 1), (rs_forward, 1, 0),
        (spread, 1, 1), (second_basis, 0), (after_first, 3), (rs_middle, 1, 0), (g_forward, 1, 2), (rs_forward, 1, 1),
        (spread, 1, 2), (ar_mid, 2), (g_forward, 1, 3), (rs_middle, 1, 1), (after_second, 0), (rs_forward, 1, 2),
        (spread, 1, 3), (second_basis, 1), (rs_middle, 1, 2), (after_second, 1), (rs_forward, 1, 3),
        (rs_middle, 1, 3), (after_second, 2), (ar_mid, 3), (after_second, 3),
        (output, 0), (ar_mid, 4), (output, 1),
    ]
    for step, *where in steps:
        step(*where)

    for copy in due.values():
        copy.wait_recv()
    for copy in sent.values():
        copy.wait_send()


def local(mobility, right_side, precond):
    mob = mobility.reshape(9, 512, 1024)
    vmem = pl.BlockSpec(memory_space=pltpu.VMEM)
    dma = pltpu.SemaphoreType.DMA
    n = BATCHES
    return pl.pallas_call(
        kernel,
        out_shape=(jax.ShapeDtypeStruct((3, 64, 512), F32), jax.ShapeDtypeStruct((3, 2, 512), F32)),
        in_specs=[pl.BlockSpec(memory_space=pl.ANY), vmem, vmem],
        out_specs=(vmem, vmem),
        scratch_shapes=[
            pltpu.VMEM((9, 512, 1024), BF16),
            pltpu.VMEM((3, 1024, 1536), BF16),
            pltpu.VMEM((2, 96, 512), F32),
            pltpu.VMEM((2, 96, 512), F32),
            pltpu.VMEM((n, 3, 4, 4, 64, LANES), F32),
            pltpu.VMEM((n, 2, 3, 4, 32, LANES), F32),
            pltpu.VMEM((2, n, 2, 6, 3, 2, 32, LANES), BF16),
            pltpu.VMEM((2, n, 2, 6, 3, 2, 32, LANES), BF16),
            pltpu.VMEM((2, n, 2, 3, 3, 32, LANES), BF16),
            pltpu.VMEM((2, n, 2, 3, 3, 32, LANES), BF16),
            pltpu.VMEM((n, 3, 8, 64, LANES), F32),
            pltpu.VMEM((2, n, 3, 8, 64, LANES), BF16),
            pltpu.VMEM((5, 16, 8, 128), F32),
            pltpu.VMEM((5, 8, 8, 128), F32),
            dma((9,)),
            dma((2, n, 2, 9)),
            dma((2, n, 2, 9)),
            dma((2, n, 7)),
            dma((2, n, 7)),
            dma((5, 2)),
            dma((5, 2)),
        ],
        compiler_params=pltpu.CompilerParams(
            collective_id=0, has_side_effects=True, vmem_limit_bytes=60 * 1024 * 1024
        ),
    )(mob, right_side, precond)


def solution(mesh):
    return jax.shard_map(
        local,
        mesh=mesh,
        in_specs=(P(None, None, None, "src", None, "tgt"), P(None, ("tgt", "src"), None), P(None, ("tgt", "src"))),
        out_specs=(P(None, ("tgt", "src"), None), P()),
        check_vma=False,
    )
```

```python
import jax
import jax.numpy as jnp
from jax import lax
from jax.experimental import pallas as pl
from jax.experimental.pallas import tpu as pltpu
from jax.sharding import PartitionSpec as P

MESH = pl.DeviceIdType.MESH
F32 = jnp.float32
BF16 = jnp.bfloat16
HIGHEST = lax.Precision.HIGHEST
LANES = 128
EPS = 1e-06


def least_squares(beta, h_one_one, h_two_one, h_one_two, h_two_two, h_three_two):
    rho_one = jnp.sqrt(h_one_one * h_one_one + h_two_one * h_two_one)
    cos_one = h_one_one / rho_one
    sin_one = h_two_one / rho_one
    g_one = cos_one * beta
    g_two = -sin_one * beta
    top = cos_one * h_one_two + sin_one * h_two_two
    low = cos_one * h_two_two - sin_one * h_one_two
    rho_two = jnp.sqrt(low * low + h_three_two * h_three_two)
    cos_two = low / rho_two
    sin_two = h_three_two / rho_two
    y_two = cos_two * g_two / rho_two
    y_one = (g_one - top * y_two) / rho_one
    return (y_one, y_two, jnp.abs(sin_two * g_two))


BATCHES = 4
WIDE = 2


def kernel(
    mob, rhs, pre, sol, arn,
    stage, mt, v1, w, o, q1, snd1, rcv1, snd2, rcv2, wide, g, ar1, ar2,
    mob_sem, rs_send, rs_recv, g_send, g_recv, ar_send, ar_recv,
):
    t = lax.axis_index("tgt")
    s = lax.axis_index("src")
    y, core = t // 2, t % 2
    z, x = s // 4, s % 4
    pos = {"z": z, "x": x}

    def at(p, k):
        return (p + k + 4) % 4

    sent, due = {}, {}

    def begin(key, out, into):
        out.start()
        sent[key], due[key] = out, into

    def arrived(key):
        due.pop(key).wait_recv()

    loads = [pltpu.make_async_copy(mob.at[j], stage.at[j], mob_sem.at[j]) for j in range(9)]
    for load in loads:
        load.start()
    barrier = pltpu.get_barrier_semaphore()
    for k in range(1, 16):
        pl.semaphore_signal(barrier, inc=1, device_id=(t, (s + k) % 16), device_id_type=MESH)
    for k in range(1, 8):
        pl.semaphore_signal(barrier, inc=1, device_id=((t + k) % 8, s), device_id_type=MESH)

    def apply_blocks(first, second):
        zeros = jnp.zeros_like(first)
        both = jnp.concatenate(
            [jnp.concatenate([first, zeros], axis=0), jnp.concatenate([zeros, second], axis=0)], axis=1
        )
        out = jnp.dot(pre[...], both, precision=HIGHEST, preferred_element_type=F32)
        n = first.shape[1]
        return out[:, :n], out[:, n:]

    def inner(a, b):
        return jnp.sum(a[0] * b[0], axis=0, keepdims=True) + jnp.sum(a[1] * b[1], axis=0, keepdims=True)

    def ar_copy1(i, slot, target):
        return pltpu.make_async_remote_copy(
            src_ref=ar1.at[i, slot], dst_ref=ar1.at[i, slot], send_sem=ar_send.at[i, 0],
            recv_sem=ar_recv.at[i, 0], device_id=(target, s), device_id_type=MESH)

    def ar_copy2(i, slot, target):
        return pltpu.make_async_remote_copy(
            src_ref=ar2.at[i, slot], dst_ref=ar2.at[i, slot], send_sem=ar_send.at[i, 1],
            recv_sem=ar_recv.at[i, 1], device_id=(t, target), device_id_type=MESH)

    def ar_start(i, rows):
        ar1[i, t] = jnp.concatenate(rows + [jnp.zeros((8 - len(rows), 128), F32)], axis=0)
        for k in range(1, 8):
            ar_copy1(i, t, (t + k) % 8).start()
        sent["a", i] = due["a", i] = ar_copy1(i, pl.ds(0, 7), (t + 1) % 8)

    def ar_mid(i):
        arrived(("a", i))
        total = ar1[i, 0]
        for k in range(1, 8):
            total = total + ar1[i, k]
        ar2[i, s] = total
        for k in range(1, 16):
            ar_copy2(i, s, (s + k) % 16).start()
        sent["b", i] = due["b", i] = ar_copy2(i, pl.ds(0, 15), (s + 1) % 16)

    def ar_end(i):
        arrived(("b", i))
        total = ar2[i, 0]
        for k in range(1, 16):
            total = total + ar2[i, k]
        return [total[k:k + 1] for k in range(8)]

    other = 1 - core
    sib = (y * 2 + other, s)

    def g_copy(op, b, i, out):
        ref = wide.at[b] if op == 0 and b < WIDE else g.at[op, b]
        if i == 0:
            part, target = (t if out else y * 2 + other), sib
        elif i < 4:
            part, target = (t if out else at(y, -i) * 2 + core), (at(y, i) * 2 + core, s)
        else:
            part, target = at(y, 3 - i) * 2 + (core if out else other), sib
        return pltpu.make_async_remote_copy(
            src_ref=ref.at[:, part], dst_ref=ref.at[:, part], send_sem=g_send.at[op, b, i],
            recv_sem=g_recv.at[op, b, i], device_id=target, device_id_type=MESH)

    def g_send_one(op, b, i):
        begin(("g", op, b, i), g_copy(op, b, i, True), g_copy(op, b, i, False))

    def g_start(op, b, vec):
        for f in range(2):
            for c in range(3):
                val = vec[f][c * 32:(c + 1) * 32]
                if op == 0 and b < WIDE:
                    wide[b, c, t, f * 32:(f + 1) * 32, :] = val
                else:
                    g[op, b, c, t, f * 32:(f + 1) * 32, :] = val.astype(BF16)
        for i in (2, 1, 3, 0):
            g_send_one(op, b, i)

    def g_forward(op, b):
        for i in (1, 3, 2):
            arrived(("g", op, b, i))
            g_send_one(op, b, i + 3)

    def g_finish(op, b):
        for i in (0, 4, 6, 5):
            arrived(("g", op, b, i))

    def multiply(op, b, n, c):
        if c == 0:
            for k in range(b, b + n):
                g_finish(op, k)
                if op == 0 and k < WIDE:
                    for c2 in range(3):
                        g[0, k, c2] = (wide[k, c2] / betas[k].reshape(1, 1, LANES)).astype(BF16)
        vec = [g[op, k].reshape(1536, LANES) for k in range(b, b + n)]
        acc = jnp.dot(mt[c], vec[0] if n == 1 else jnp.concatenate(vec, axis=1), preferred_element_type=F32)
        for k in range(n):
            o[b + k, c] = acc[:, k * LANES:(k + 1) * LANES].reshape(4, 4, 64, LANES)

    order = (("z", "x"), ("x", "z"))

    def device(ring, k):
        if ring == "z":
            return (t, at(z, k) * 4 + x)
        return (t, z * 4 + at(x, k))

    def rs_send_one(op, b, fl, m, val):
        if m < 6:
            snd, rcv = snd1.at[op, b, fl, m], rcv1.at[op, b, fl, m]
            target = device(order[fl][0], 1 - 2 * (m // 3))
        else:
            snd, rcv = snd2.at[op, b, fl, m - 6], rcv2.at[op, b, fl, m - 6]
            target = device(order[fl][1], m - 5)
        snd[...] = val.astype(BF16)
        copy = pltpu.make_async_remote_copy(
            src_ref=snd, dst_ref=rcv, send_sem=rs_send.at[op, b, fl, m], recv_sem=rs_recv.at[op, b, fl, m],
            device_id=target, device_id_type=MESH)
        begin(("r", op, b, fl, m), copy, copy)

    def own(b, fl, k, half):
        grp = at(pos[order[fl][0]], k)
        if fl == 0:
            return o[b, :, grp, half * 2:half * 2 + 2, 0:32]
        return o[b, :, half * 2:half * 2 + 2, grp, 32:64]

    def rs_first(op, b):
        for d in range(2):
            for fl in range(2):
                rs_send_one(op, b, fl, d * 3, own(b, fl, 2, d))
        for d in range(2):
            for fl in range(2):
                rs_send_one(op, b, fl, d * 3 + 1, own(b, fl, 1 - 2 * d, 1 - d))

    def rs_forward(op, b):
        for d in range(2):
            for fl in range(2):
                arrived(("r", op, b, fl, d * 3))
                rs_send_one(op, b, fl, d * 3 + 2, own(b, fl, 1 - 2 * d, d) + rcv1[op, b, fl, d * 3].astype(F32))

    def rs_middle(op, b):
        for fl in range(2):
            for m in (1, 4, 2, 5):
                arrived(("r", op, b, fl, m))
            for half in range(2):
                q1[b, fl, :, half * 2:half * 2 + 2] = (
                    own(b, fl, 0, half) + rcv1[op, b, fl, 2 - half].astype(F32) + rcv1[op, b, fl, 4 + half].astype(F32)
                )
            for k in (2, 1, 3):
                rs_send_one(op, b, fl, 5 + k, q1[b, fl, :, at(pos[order[fl][1]], k)])

    def rs_end(op, b):
        out = []
        for fl in range(2):
            total = q1[b, fl, :, pos[order[fl][1]]]
            for k in (1, 3, 2):
                arrived(("r", op, b, fl, 5 + k))
                total = total + rcv2[op, b, fl, k - 1].astype(F32)
            out.append(total.reshape(96, LANES))
        return out

    def cols(b):
        return slice(b * LANES, (b + 1) * LANES)

    def get(ref, b):
        return [ref[f, :, cols(b)] for f in range(2)]

    eye = (
        lax.broadcasted_iota(jnp.int32, (256, 256), 0) == lax.broadcasted_iota(jnp.int32, (256, 256), 1)
    ).astype(F32).astype(BF16)

    def turn(j):
        loads[j].wait()
        c2, c = j // 3, j % 3

        def block(i, carry):
            cut = pl.ds(pl.multiple_of(i * 256, 256), 256)
            for kb in range(2):
                tile = stage[j, kb * 256:(kb + 1) * 256, cut]
                turned = lax.dot_general(eye, tile, (((1,), (1,)), ((), ())), preferred_element_type=F32)
                mt[c, cut, c2 * 512 + kb * 256:c2 * 512 + (kb + 1) * 256] = turned.astype(BF16)
            return carry

        lax.fori_loop(0, 4, block, 0)

    def fiber(f):
        return jnp.concatenate([rhs[c, f * 32:(f + 1) * 32, :] for c in range(3)], axis=0)

    def start():
        r0 = apply_blocks(fiber(0), fiber(1))
        for f in range(2):
            v1[f] = r0[f]

    def greeted():
        pl.semaphore_wait(barrier, 22)
        ar_start(0, [inner(get(v1, b), get(v1, b)) for b in range(BATCHES)])
        for b in range(WIDE):
            g_start(0, b, get(v1, b))

    betas, squares = [None] * BATCHES, [None] * BATCHES
    h11, h21, n22 = [None] * BATCHES, [None] * BATCHES, [None] * BATCHES
    kept = {}

    def first_basis():
        tile = ar_end(0)
        for b in range(BATCHES):
            squares[b] = tile[b]
            betas[b] = jnp.sqrt(tile[b] + EPS)
            for f in range(2):
                v1[f, :, cols(b)] = v1[f, :, cols(b)] / betas[b]
            if b >= WIDE:
                g_start(0, b, get(v1, b))

    def after_first(b):
        kv = rs_end(0, b)
        vec = get(v1, b)
        wv = apply_blocks(vec[0] + kv[0], vec[1] + kv[1])
        for f in range(2):
            w[f, :, cols(b)] = wv[f]
        g_start(1, b, wv)
        kept[b] = [inner(vec, wv), inner(wv, wv)]
        if b % 2 == 1:
            ar_start(1 + b // 2, kept[b - 1] + kept[b])

    def second_basis(pair):
        tile = ar_end(1 + pair)
        for j in range(2):
            b = pair * 2 + j
            h, ww = tile[j * 2], tile[j * 2 + 1]
            n11 = squares[b] / (squares[b] + EPS)
            left = jnp.maximum(ww - h * h * (2.0 - n11), 0.0)
            h11[b] = h
            h21[b] = jnp.sqrt(left + EPS)
            n22[b] = left / (left + EPS)

    def after_second(b):
        kw = rs_end(1, b)
        first, wv = get(v1, b), get(w, b)
        q = apply_blocks(wv[0] + kw[0], wv[1] + kw[1])
        second = [(wv[f] - h11[b] * first[f]) / h21[b] for f in range(2)]
        zv = [(q[f] - h11[b] * wv[f]) / h21[b] for f in range(2)]
        for f in range(2):
            w[f, :, cols(b)] = second[f]
        kept[b] = [inner(first, zv), inner(second, zv), inner(zv, zv)]
        if b % 2 == 1:
            ar_start(3 + b // 2, kept[b - 1] + kept[b])

    def output(pair):
        tile = ar_end(3 + pair)
        for j in range(2):
            b = pair * 2 + j
            h12, h22, zz = tile[j * 3:j * 3 + 3]
            n11 = squares[b] / (squares[b] + EPS)
            n12 = h11[b] * (1.0 - n11) / h21[b]
            left = zz - h12 * h12 * (2.0 - n11) - h22 * h22 * (2.0 - n22[b]) + 2.0 * h12 * h22 * n12
            h32 = jnp.sqrt(jnp.maximum(left, 0.0) + EPS)
            y1, y2, estimate = least_squares(betas[b], h11[b], h21[b], h12, h22, h32)
            for f in range(2):
                out = y1 * v1[f, :, cols(b)] + y2 * w[f, :, cols(b)]
                for c in range(3):
                    sol[c, f * 32:(f + 1) * 32, cols(b)] = out[c * 32:(c + 1) * 32]
            for i, row in enumerate(((h11[b], h12), (h21[b], h22), (estimate, h32))):
                for k in range(2):
                    arn[i, k:k + 1, cols(b)] = row[k]

    steps = [
        (start,), (turn, 0), (turn, 1), (turn, 2), (turn, 3), (turn, 4), (turn, 5), (greeted,), (turn, 6), (turn, 7),
        (turn, 8), (ar_mid, 0), (g_forward, 0, 0), (first_basis,), (multiply, 0, 0, 1, 0), (multiply, 0, 0, 1, 1),
        (g_forward, 0, 1), (multiply, 0, 0, 1, 2), (rs_first, 0, 0), (g_forward, 0, 2), (multiply, 0, 1, 1, 0),
        (multiply, 0, 1, 1, 1), (g_forward, 0, 3), (rs_forward, 0, 0), (multiply, 0, 1, 1, 2), (rs_first, 0, 1),
        (multiply, 0, 2, 2, 0), (multiply, 0, 2, 2, 1), (rs_middle, 0, 0), (rs_forward, 0, 1),
        (multiply, 0, 2, 2, 2), (rs_first, 0, 2), (rs_first, 0, 3), (after_first, 0), (rs_middle, 0, 1),
        (rs_forward, 0, 2), (rs_forward, 0, 3), (g_forward, 1, 0), (multiply, 1, 0, 1, 0), (rs_middle, 0, 2),
        (after_first, 1), (rs_middle, 0, 3), (multiply, 1, 0, 1, 1), (multiply, 1, 0, 1, 2), (after_first, 2),
        (rs_first, 1, 0), (g_forward, 1, 1), (after_first, 3), (ar_mid, 1), (multiply, 1, 1, 1, 0),
        (rs_forward, 1, 0), (g_forward, 1, 2), (multiply, 1, 1, 1, 1), (multiply, 1, 1, 1, 2), (g_forward, 1, 3),
        (rs_first, 1, 1), (rs_middle, 1, 0), (ar_mid, 2), (second_basis, 0), (multiply, 1, 2, 2, 0),
        (multiply, 1, 2, 2, 1), (rs_forward, 1, 1), (multiply, 1, 2, 2, 2), (rs_first, 1, 3), (after_second, 0),
        (rs_first, 1, 2), (rs_middle, 1, 1), (second_basis, 1), (rs_forward, 1, 3), (rs_forward, 1, 2),
        (after_second, 1), (rs_middle, 1, 3), (rs_middle, 1, 2), (ar_mid, 3), (after_second, 2), (after_second, 3),
        (output, 0), (ar_mid, 4), (output, 1),
    ]
    for step, *where in steps:
        step(*where)

    for copy in due.values():
        copy.wait_recv()
    for copy in sent.values():
        copy.wait_send()


def local(mobility, right_side, precond):
    mob = mobility.reshape(9, 512, 1024)
    vmem = pl.BlockSpec(memory_space=pltpu.VMEM)
    dma = pltpu.SemaphoreType.DMA
    n = BATCHES
    return pl.pallas_call(
        kernel,
        out_shape=(jax.ShapeDtypeStruct((3, 64, 512), F32), jax.ShapeDtypeStruct((3, 2, 512), F32)),
        in_specs=[pl.BlockSpec(memory_space=pl.ANY), vmem, vmem],
        out_specs=(vmem, vmem),
        scratch_shapes=[
            pltpu.VMEM((9, 512, 1024), BF16),
            pltpu.VMEM((3, 1024, 1536), BF16),
            pltpu.VMEM((2, 96, 512), F32),
            pltpu.VMEM((2, 96, 512), F32),
            pltpu.VMEM((n, 3, 4, 4, 64, LANES), F32),
            pltpu.VMEM((n, 2, 3, 4, 32, LANES), F32),
            pltpu.VMEM((2, n, 2, 6, 3, 2, 32, LANES), BF16),
            pltpu.VMEM((2, n, 2, 6, 3, 2, 32, LANES), BF16),
            pltpu.VMEM((2, n, 2, 3, 3, 32, LANES), BF16),
            pltpu.VMEM((2, n, 2, 3, 3, 32, LANES), BF16),
            pltpu.VMEM((WIDE, 3, 8, 64, LANES), F32),
            pltpu.VMEM((2, n, 3, 8, 64, LANES), BF16),
            pltpu.VMEM((5, 8, 8, 128), F32),
            pltpu.VMEM((5, 16, 8, 128), F32),
            dma((9,)),
            dma((2, n, 2, 9)),
            dma((2, n, 2, 9)),
            dma((2, n, 7)),
            dma((2, n, 7)),
            dma((5, 2)),
            dma((5, 2)),
        ],
        compiler_params=pltpu.CompilerParams(
            collective_id=0, has_side_effects=True, vmem_limit_bytes=60 * 1024 * 1024
        ),
    )(mob, right_side, precond)


def solution(mesh):
    return jax.shard_map(
        local,
        mesh=mesh,
        in_specs=(P(None, None, None, "src", None, "tgt"), P(None, ("tgt", "src"), None), P(None, ("tgt", "src"))),
        out_specs=(P(None, ("tgt", "src"), None), P()),
        check_vma=False,
    )
```

```python
import jax
import jax.numpy as jnp
from jax import lax
from jax.experimental import pallas as pl
from jax.experimental.pallas import tpu as pltpu
from jax.sharding import PartitionSpec as P

MESH = pl.DeviceIdType.MESH
F32 = jnp.float32
BF16 = jnp.bfloat16
HIGHEST = lax.Precision.HIGHEST
LANES = 128
EPS = 1e-06


def least_squares(beta, h_one_one, h_two_one, h_one_two, h_two_two, h_three_two):
    rho_one = jnp.sqrt(h_one_one * h_one_one + h_two_one * h_two_one)
    cos_one = h_one_one / rho_one
    sin_one = h_two_one / rho_one
    g_one = cos_one * beta
    g_two = -sin_one * beta
    top = cos_one * h_one_two + sin_one * h_two_two
    low = cos_one * h_two_two - sin_one * h_one_two
    rho_two = jnp.sqrt(low * low + h_three_two * h_three_two)
    cos_two = low / rho_two
    sin_two = h_three_two / rho_two
    y_two = cos_two * g_two / rho_two
    y_one = (g_one - top * y_two) / rho_one
    return (y_one, y_two, jnp.abs(sin_two * g_two))


BATCHES = 4
WIDE = 2


def kernel(
    mob, rhs_hbm, pre_hbm, sol, arn,
    stage, rhs, pre, mt, v1, w, o, q1, snd1, rcv1, snd2, rcv2, wide, g, ar1, ar2,
    mob_sem, in_sem, rs_send, rs_recv, g_send, g_recv, ar_send, ar_recv,
):
    t = lax.axis_index("tgt")
    s = lax.axis_index("src")
    y, core = t // 2, t % 2
    z, x = s // 4, s % 4
    pos = {"z": z, "x": x}

    def at(p, k):
        return (p + k + 4) % 4

    sent, due = {}, {}

    def begin(key, out, into):
        out.start()
        sent[key], due[key] = out, into

    def arrived(key):
        due.pop(key).wait_recv()

    barrier = pltpu.get_barrier_semaphore()
    for k in range(1, 16):
        pl.semaphore_signal(barrier, inc=1, device_id=(t, (s + k) % 16), device_id_type=MESH)
    for k in range(1, 8):
        pl.semaphore_signal(barrier, inc=1, device_id=((t + k) % 8, s), device_id_type=MESH)

    small = [
        pltpu.make_async_copy(rhs_hbm, rhs, in_sem.at[0]),
        pltpu.make_async_copy(pre_hbm, pre, in_sem.at[1]),
    ]
    loads = [pltpu.make_async_copy(mob.at[j], stage.at[j], mob_sem.at[j]) for j in range(9)]
    for load in small + [loads[j] for c in range(3) for j in range(c, 9, 3)]:
        load.start()

    def apply_blocks(first, second):
        zeros = jnp.zeros_like(first)
        both = jnp.concatenate(
            [jnp.concatenate([first, zeros], axis=0), jnp.concatenate([zeros, second], axis=0)], axis=1
        )
        out = jnp.dot(pre[...], both, precision=HIGHEST, preferred_element_type=F32)
        n = first.shape[1]
        return out[:, :n], out[:, n:]

    def inner(a, b):
        return jnp.sum(a[0] * b[0], axis=0, keepdims=True) + jnp.sum(a[1] * b[1], axis=0, keepdims=True)

    def ar_copy1(i, slot, target):
        return pltpu.make_async_remote_copy(
            src_ref=ar1.at[i, slot], dst_ref=ar1.at[i, slot], send_sem=ar_send.at[i, 0],
            recv_sem=ar_recv.at[i, 0], device_id=(target, s), device_id_type=MESH)

    def ar_copy2(i, slot, target):
        return pltpu.make_async_remote_copy(
            src_ref=ar2.at[i, slot], dst_ref=ar2.at[i, slot], send_sem=ar_send.at[i, 1],
            recv_sem=ar_recv.at[i, 1], device_id=(t, target), device_id_type=MESH)

    def ar_start(i, rows):
        ar1[i, t] = jnp.concatenate(rows + [jnp.zeros((8 - len(rows), 128), F32)], axis=0)
        for k in range(1, 8):
            ar_copy1(i, t, (t + k) % 8).start()
        sent["a", i] = due["a", i] = ar_copy1(i, pl.ds(0, 7), (t + 1) % 8)

    def ar_mid(i):
        arrived(("a", i))
        total = ar1[i, 0]
        for k in range(1, 8):
            total = total + ar1[i, k]
        ar2[i, s] = total
        for k in range(1, 16):
            ar_copy2(i, s, (s + k) % 16).start()
        sent["b", i] = due["b", i] = ar_copy2(i, pl.ds(0, 15), (s + 1) % 16)

    def ar_end(i):
        arrived(("b", i))
        total = ar2[i, 0]
        for k in range(1, 16):
            total = total + ar2[i, k]
        return [total[k:k + 1] for k in range(8)]

    other = 1 - core
    sib = (y * 2 + other, s)

    def g_copy(op, b, i, out):
        ref = wide.at[b] if op == 0 and b < WIDE else g.at[op, b]
        if i == 0:
            part, target = (t if out else y * 2 + other), sib
        elif i < 4:
            part, target = (t if out else at(y, -i) * 2 + core), (at(y, i) * 2 + core, s)
        else:
            part, target = at(y, 3 - i) * 2 + (core if out else other), sib
        return pltpu.make_async_remote_copy(
            src_ref=ref.at[:, part], dst_ref=ref.at[:, part], send_sem=g_send.at[op, b, i],
            recv_sem=g_recv.at[op, b, i], device_id=target, device_id_type=MESH)

    def g_send_one(op, b, i):
        begin(("g", op, b, i), g_copy(op, b, i, True), g_copy(op, b, i, False))

    def g_start(op, b, vec):
        for f in range(2):
            for c in range(3):
                val = vec[f][c * 32:(c + 1) * 32]
                if op == 0 and b < WIDE:
                    wide[b, c, t, f * 32:(f + 1) * 32, :] = val
                else:
                    g[op, b, c, t, f * 32:(f + 1) * 32, :] = val.astype(BF16)
        for i in (2, 1, 3, 0):
            g_send_one(op, b, i)

    def g_forward(op, b):
        for i in (1, 3, 2):
            arrived(("g", op, b, i))
            g_send_one(op, b, i + 3)

    def g_finish(op, b):
        for i in (0, 4, 6, 5):
            arrived(("g", op, b, i))

    def multiply(op, b, n, c):
        if c == 0:
            for k in range(b, b + n):
                g_finish(op, k)
                if op == 0 and k < WIDE:
                    for c2 in range(3):
                        g[0, k, c2] = (wide[k, c2] / betas[k].reshape(1, 1, LANES)).astype(BF16)
        vec = [g[op, k].reshape(1536, LANES) for k in range(b, b + n)]
        acc = jnp.dot(mt[c], vec[0] if n == 1 else jnp.concatenate(vec, axis=1), preferred_element_type=F32)
        for k in range(n):
            o[b + k, c] = acc[:, k * LANES:(k + 1) * LANES].reshape(4, 4, 64, LANES)

    order = (("z", "x"), ("x", "z"))

    def device(ring, k):
        if ring == "z":
            return (t, at(z, k) * 4 + x)
        return (t, z * 4 + at(x, k))

    def rs_send_one(op, b, fl, m, val):
        if m < 6:
            snd, rcv = snd1.at[op, b, fl, m], rcv1.at[op, b, fl, m]
            target = device(order[fl][0], 1 - 2 * (m // 3))
        else:
            snd, rcv = snd2.at[op, b, fl, m - 6], rcv2.at[op, b, fl, m - 6]
            target = device(order[fl][1], m - 5)
        snd[...] = val.astype(BF16)
        copy = pltpu.make_async_remote_copy(
            src_ref=snd, dst_ref=rcv, send_sem=rs_send.at[op, b, fl, m], recv_sem=rs_recv.at[op, b, fl, m],
            device_id=target, device_id_type=MESH)
        begin(("r", op, b, fl, m), copy, copy)

    def own(b, fl, k, half):
        grp = at(pos[order[fl][0]], k)
        if fl == 0:
            return o[b, :, grp, half * 2:half * 2 + 2, 0:32]
        return o[b, :, half * 2:half * 2 + 2, grp, 32:64]

    def rs_first(op, b):
        for d in range(2):
            for fl in range(2):
                rs_send_one(op, b, fl, d * 3, own(b, fl, 2, d))
        for d in range(2):
            for fl in range(2):
                rs_send_one(op, b, fl, d * 3 + 1, own(b, fl, 1 - 2 * d, 1 - d))

    def rs_forward(op, b):
        for d in range(2):
            for fl in range(2):
                arrived(("r", op, b, fl, d * 3))
                rs_send_one(op, b, fl, d * 3 + 2, own(b, fl, 1 - 2 * d, d) + rcv1[op, b, fl, d * 3].astype(F32))

    def rs_middle(op, b):
        for fl in range(2):
            for m in (1, 4, 2, 5):
                arrived(("r", op, b, fl, m))
            for half in range(2):
                q1[b, fl, :, half * 2:half * 2 + 2] = (
                    own(b, fl, 0, half) + rcv1[op, b, fl, 2 - half].astype(F32) + rcv1[op, b, fl, 4 + half].astype(F32)
                )
            for k in (2, 1, 3):
                rs_send_one(op, b, fl, 5 + k, q1[b, fl, :, at(pos[order[fl][1]], k)])

    def rs_end(op, b):
        out = []
        for fl in range(2):
            total = q1[b, fl, :, pos[order[fl][1]]]
            for k in (1, 3, 2):
                arrived(("r", op, b, fl, 5 + k))
                total = total + rcv2[op, b, fl, k - 1].astype(F32)
            out.append(total.reshape(96, LANES))
        return out

    def cols(b):
        return slice(b * LANES, (b + 1) * LANES)

    def get(ref, b):
        return [ref[f, :, cols(b)] for f in range(2)]

    eye = (
        lax.broadcasted_iota(jnp.int32, (256, 256), 0) == lax.broadcasted_iota(jnp.int32, (256, 256), 1)
    ).astype(F32).astype(BF16)

    def turn(j):
        loads[j].wait()
        c2, c = j // 3, j % 3

        def block(i, carry):
            cut = pl.ds(pl.multiple_of(i * 256, 256), 256)
            for kb in range(2):
                tile = stage[j, kb * 256:(kb + 1) * 256, cut]
                turned = lax.dot_general(eye, tile, (((1,), (1,)), ((), ())), preferred_element_type=F32)
                mt[c, cut, c2 * 512 + kb * 256:c2 * 512 + (kb + 1) * 256] = turned.astype(BF16)
            return carry

        lax.fori_loop(0, 4, block, 0)

    def fiber(f):
        return jnp.concatenate([rhs[c, f * 32:(f + 1) * 32, :] for c in range(3)], axis=0)

    def start():
        for load in small:
            load.wait()
        r0 = apply_blocks(fiber(0), fiber(1))
        for f in range(2):
            v1[f] = r0[f]

    def greeted():
        pl.semaphore_wait(barrier, 22)
        ar_start(0, [inner(get(v1, b), get(v1, b)) for b in range(BATCHES)])
        for b in range(WIDE):
            g_start(0, b, get(v1, b))

    betas, squares = [None] * BATCHES, [None] * BATCHES
    h11, h21, n22 = [None] * BATCHES, [None] * BATCHES, [None] * BATCHES
    kept = {}

    def first_basis():
        tile = ar_end(0)
        for b in range(BATCHES):
            squares[b] = tile[b]
            betas[b] = jnp.sqrt(tile[b] + EPS)
            for f in range(2):
                v1[f, :, cols(b)] = v1[f, :, cols(b)] / betas[b]
            if b >= WIDE:
                g_start(0, b, get(v1, b))

    def after_first(b):
        kv = rs_end(0, b)
        vec = get(v1, b)
        wv = apply_blocks(vec[0] + kv[0], vec[1] + kv[1])
        for f in range(2):
            w[f, :, cols(b)] = wv[f]
        g_start(1, b, wv)
        kept[b] = [inner(vec, wv), inner(wv, wv)]
        if b % 2 == 1:
            ar_start(1 + b // 2, kept[b - 1] + kept[b])

    def second_basis(pair):
        tile = ar_end(1 + pair)
        for j in range(2):
            b = pair * 2 + j
            h, ww = tile[j * 2], tile[j * 2 + 1]
            n11 = squares[b] / (squares[b] + EPS)
            left = jnp.maximum(ww - h * h * (2.0 - n11), 0.0)
            h11[b] = h
            h21[b] = jnp.sqrt(left + EPS)
            n22[b] = left / (left + EPS)

    def after_second(b):
        kw = rs_end(1, b)
        first, wv = get(v1, b), get(w, b)
        q = apply_blocks(wv[0] + kw[0], wv[1] + kw[1])
        second = [(wv[f] - h11[b] * first[f]) / h21[b] for f in range(2)]
        zv = [(q[f] - h11[b] * wv[f]) / h21[b] for f in range(2)]
        for f in range(2):
            w[f, :, cols(b)] = second[f]
        kept[b] = [inner(first, zv), inner(second, zv), inner(zv, zv)]
        if b % 2 == 1:
            ar_start(3 + b // 2, kept[b - 1] + kept[b])

    def output(pair):
        tile = ar_end(3 + pair)
        for j in range(2):
            b = pair * 2 + j
            h12, h22, zz = tile[j * 3:j * 3 + 3]
            n11 = squares[b] / (squares[b] + EPS)
            n12 = h11[b] * (1.0 - n11) / h21[b]
            left = zz - h12 * h12 * (2.0 - n11) - h22 * h22 * (2.0 - n22[b]) + 2.0 * h12 * h22 * n12
            h32 = jnp.sqrt(jnp.maximum(left, 0.0) + EPS)
            y1, y2, estimate = least_squares(betas[b], h11[b], h21[b], h12, h22, h32)
            for f in range(2):
                out = y1 * v1[f, :, cols(b)] + y2 * w[f, :, cols(b)]
                for c in range(3):
                    sol[c, f * 32:(f + 1) * 32, cols(b)] = out[c * 32:(c + 1) * 32]
            for i, row in enumerate(((h11[b], h12), (h21[b], h22), (estimate, h32))):
                for k in range(2):
                    arn[i, k:k + 1, cols(b)] = row[k]

    steps = [
        (start,), (greeted,), (turn, 0), (turn, 3), (turn, 6), (turn, 1), (ar_mid, 0), (turn, 4), (turn, 7),
        (turn, 2), (g_forward, 0, 0), (turn, 5), (turn, 8), (first_basis,), (multiply, 0, 0, 1, 0),
        (g_forward, 0, 1), (multiply, 0, 0, 1, 1), (multiply, 0, 0, 1, 2), (rs_first, 0, 0), (g_forward, 0, 2),
        (multiply, 0, 1, 2, 0), (g_forward, 0, 3), (rs_forward, 0, 0), (multiply, 0, 1, 2, 1),
        (multiply, 0, 1, 2, 2), (rs_first, 0, 1), (multiply, 0, 3, 1, 0), (rs_middle, 0, 0), (rs_first, 0, 2),
        (multiply, 0, 3, 1, 1), (rs_forward, 0, 1), (multiply, 0, 3, 1, 2), (rs_first, 0, 3), (after_first, 0),
        (rs_forward, 0, 2), (rs_middle, 0, 1), (rs_forward, 0, 3), (g_forward, 1, 0), (rs_middle, 0, 2),
        (multiply, 1, 0, 1, 0), (after_first, 1), (rs_middle, 0, 3), (multiply, 1, 0, 1, 1), (after_first, 2),
        (multiply, 1, 0, 1, 2), (rs_first, 1, 0), (g_forward, 1, 1), (after_first, 3), (ar_mid, 1),
        (multiply, 1, 1, 1, 0), (rs_forward, 1, 0), (g_forward, 1, 2), (multiply, 1, 1, 1, 1),
        (multiply, 1, 1, 1, 2), (g_forward, 1, 3), (rs_first, 1, 1), (ar_mid, 2), (rs_middle, 1, 0),
        (multiply, 1, 2, 2, 0), (multiply, 1, 2, 2, 1), (rs_forward, 1, 1), (second_basis, 0),
        (multiply, 1, 2, 2, 2), (rs_first, 1, 2), (rs_first, 1, 3), (after_second, 0), (second_basis, 1),
        (rs_middle, 1, 1), (rs_forward, 1, 2), (rs_forward, 1, 3), (after_second, 1), (rs_middle, 1, 2),
        (rs_middle, 1, 3), (ar_mid, 3), (after_second, 2), (after_second, 3), (output, 0), (ar_mid, 4), (output, 1),
    ]
    for step, *where in steps:
        step(*where)

    for copy in due.values():
        copy.wait_recv()
    for copy in sent.values():
        copy.wait_send()


def local(mobility, right_side, precond):
    mob = mobility.reshape(9, 512, 1024)
    vmem = pl.BlockSpec(memory_space=pltpu.VMEM)
    dma = pltpu.SemaphoreType.DMA
    n = BATCHES
    return pl.pallas_call(
        kernel,
        out_shape=(jax.ShapeDtypeStruct((3, 64, 512), F32), jax.ShapeDtypeStruct((3, 2, 512), F32)),
        in_specs=[pl.BlockSpec(memory_space=pl.ANY)] * 3,
        out_specs=(vmem, vmem),
        scratch_shapes=[
            pltpu.VMEM((9, 512, 1024), BF16),
            pltpu.VMEM((3, 64, 512), F32),
            pltpu.VMEM((96, 192), F32),
            pltpu.VMEM((3, 1024, 1536), BF16),
            pltpu.VMEM((2, 96, 512), F32),
            pltpu.VMEM((2, 96, 512), F32),
            pltpu.VMEM((n, 3, 4, 4, 64, LANES), F32),
            pltpu.VMEM((n, 2, 3, 4, 32, LANES), F32),
            pltpu.VMEM((2, n, 2, 6, 3, 2, 32, LANES), BF16),
            pltpu.VMEM((2, n, 2, 6, 3, 2, 32, LANES), BF16),
            pltpu.VMEM((2, n, 2, 3, 3, 32, LANES), BF16),
            pltpu.VMEM((2, n, 2, 3, 3, 32, LANES), BF16),
            pltpu.VMEM((WIDE, 3, 8, 64, LANES), F32),
            pltpu.VMEM((2, n, 3, 8, 64, LANES), BF16),
            pltpu.VMEM((5, 8, 8, 128), F32),
            pltpu.VMEM((5, 16, 8, 128), F32),
            dma((9,)),
            dma((2,)),
            dma((2, n, 2, 9)),
            dma((2, n, 2, 9)),
            dma((2, n, 7)),
            dma((2, n, 7)),
            dma((5, 2)),
            dma((5, 2)),
        ],
        compiler_params=pltpu.CompilerParams(
            collective_id=0, has_side_effects=True, vmem_limit_bytes=60 * 1024 * 1024
        ),
    )(mob, right_side, precond)


def solution(mesh):
    return jax.shard_map(
        local,
        mesh=mesh,
        in_specs=(P(None, None, None, "src", None, "tgt"), P(None, ("tgt", "src"), None), P(None, ("tgt", "src"))),
        out_specs=(P(None, ("tgt", "src"), None), P()),
        check_vma=False,
    )
```

```python
import jax
import jax.numpy as jnp
from jax import lax
from jax.experimental import pallas as pl
from jax.experimental.pallas import tpu as pltpu
from jax.sharding import PartitionSpec as P

MESH = pl.DeviceIdType.MESH
F32 = jnp.float32
BF16 = jnp.bfloat16
HIGHEST = lax.Precision.HIGHEST
LANES = 128
EPS = 1e-06


def least_squares(beta, h_one_one, h_two_one, h_one_two, h_two_two, h_three_two):
    rho_one = jnp.sqrt(h_one_one * h_one_one + h_two_one * h_two_one)
    cos_one = h_one_one / rho_one
    sin_one = h_two_one / rho_one
    g_one = cos_one * beta
    g_two = -sin_one * beta
    top = cos_one * h_one_two + sin_one * h_two_two
    low = cos_one * h_two_two - sin_one * h_one_two
    rho_two = jnp.sqrt(low * low + h_three_two * h_three_two)
    cos_two = low / rho_two
    sin_two = h_three_two / rho_two
    y_two = cos_two * g_two / rho_two
    y_one = (g_one - top * y_two) / rho_one
    return (y_one, y_two, jnp.abs(sin_two * g_two))


BATCHES = 4
WIDE = 2


def kernel(
    mob, rhs_hbm, pre_hbm, sol, arn,
    stage, rhs, pre, mt, v1, w, o, q1, snd1, rcv1, snd2, rcv2, wide, g, ar1, ar2,
    mob_sem, in_sem, rs_send, rs_recv, g_send, g_recv, ar_send, ar_recv,
):
    t = lax.axis_index("tgt")
    s = lax.axis_index("src")
    y, core = t // 2, t % 2
    z, x = s // 4, s % 4
    pos = {"z": z, "x": x}

    def at(p, k):
        return (p + k + 4) % 4

    sent, due = {}, {}

    def begin(key, out, into):
        out.start()
        sent[key], due[key] = out, into

    def arrived(key):
        due.pop(key).wait_recv()

    barrier = pltpu.get_barrier_semaphore()
    for k in range(1, 16):
        pl.semaphore_signal(barrier, inc=1, device_id=(t, (s + k) % 16), device_id_type=MESH)
    for k in range(1, 8):
        pl.semaphore_signal(barrier, inc=1, device_id=((t + k) % 8, s), device_id_type=MESH)

    small = [
        pltpu.make_async_copy(rhs_hbm, rhs, in_sem.at[0]),
        pltpu.make_async_copy(pre_hbm, pre, in_sem.at[1]),
    ]
    loads = [pltpu.make_async_copy(mob.at[j], stage.at[j], mob_sem.at[j]) for j in range(9)]
    for load in small + [loads[j] for c in range(3) for j in range(c, 9, 3)]:
        load.start()

    def apply_blocks(first, second):
        zeros = jnp.zeros_like(first)
        both = jnp.concatenate(
            [jnp.concatenate([first, zeros], axis=0), jnp.concatenate([zeros, second], axis=0)], axis=1
        )
        out = jnp.dot(pre[...], both, precision=HIGHEST, preferred_element_type=F32)
        n = first.shape[1]
        return out[:, :n], out[:, n:]

    def inner(a, b):
        return jnp.sum(a[0] * b[0], axis=0, keepdims=True) + jnp.sum(a[1] * b[1], axis=0, keepdims=True)

    def ar_copy1(i, slot, target):
        return pltpu.make_async_remote_copy(
            src_ref=ar1.at[i, slot], dst_ref=ar1.at[i, slot], send_sem=ar_send.at[i, 0],
            recv_sem=ar_recv.at[i, 0], device_id=(target, s), device_id_type=MESH)

    def ar_copy2(i, slot, target):
        return pltpu.make_async_remote_copy(
            src_ref=ar2.at[i, slot], dst_ref=ar2.at[i, slot], send_sem=ar_send.at[i, 1],
            recv_sem=ar_recv.at[i, 1], device_id=(t, target), device_id_type=MESH)

    def ar_own(i, rows):
        ar1[i, t] = jnp.concatenate(rows + [jnp.zeros((8 - len(rows), 128), F32)], axis=0)

    def ar_start(i, rows=None):
        if rows is not None:
            ar_own(i, rows)
        for k in range(1, 8):
            ar_copy1(i, t, (t + k) % 8).start()
        sent["a", i] = due["a", i] = ar_copy1(i, pl.ds(0, 7), (t + 1) % 8)

    def ar_mid(i):
        arrived(("a", i))
        total = ar1[i, 0]
        for k in range(1, 8):
            total = total + ar1[i, k]
        ar2[i, s] = total
        for k in range(1, 16):
            ar_copy2(i, s, (s + k) % 16).start()
        sent["b", i] = due["b", i] = ar_copy2(i, pl.ds(0, 15), (s + 1) % 16)

    def ar_end(i):
        arrived(("b", i))
        total = ar2[i, 0]
        for k in range(1, 16):
            total = total + ar2[i, k]
        return [total[k:k + 1] for k in range(8)]

    other = 1 - core
    sib = (y * 2 + other, s)

    def g_copy(op, b, i, out):
        ref = wide.at[b] if op == 0 and b < WIDE else g.at[op, b]
        if i == 0:
            part, target = (t if out else y * 2 + other), sib
        elif i < 4:
            part, target = (t if out else at(y, -i) * 2 + core), (at(y, i) * 2 + core, s)
        else:
            part, target = at(y, 3 - i) * 2 + (core if out else other), sib
        return pltpu.make_async_remote_copy(
            src_ref=ref.at[:, part], dst_ref=ref.at[:, part], send_sem=g_send.at[op, b, i],
            recv_sem=g_recv.at[op, b, i], device_id=target, device_id_type=MESH)

    def g_send_one(op, b, i):
        begin(("g", op, b, i), g_copy(op, b, i, True), g_copy(op, b, i, False))

    def g_own(op, b, vec):
        for f in range(2):
            for c in range(3):
                val = vec[f][c * 32:(c + 1) * 32]
                if op == 0 and b < WIDE:
                    wide[b, c, t, f * 32:(f + 1) * 32, :] = val
                else:
                    g[op, b, c, t, f * 32:(f + 1) * 32, :] = val.astype(BF16)

    def g_start(op, b, vec=None):
        if vec is not None:
            g_own(op, b, vec)
        for i in (2, 1, 3, 0):
            g_send_one(op, b, i)

    def g_forward(op, b):
        for i in (1, 3, 2):
            arrived(("g", op, b, i))
            g_send_one(op, b, i + 3)

    def g_finish(op, b):
        for i in (0, 4, 6, 5):
            arrived(("g", op, b, i))

    def multiply(op, b, n, c):
        if c == 0:
            for k in range(b, b + n):
                g_finish(op, k)
                if op == 0 and k < WIDE:
                    for c2 in range(3):
                        g[0, k, c2] = (wide[k, c2] / betas[k].reshape(1, 1, LANES)).astype(BF16)
        vec = [g[op, k].reshape(1536, LANES) for k in range(b, b + n)]
        acc = jnp.dot(mt[c], vec[0] if n == 1 else jnp.concatenate(vec, axis=1), preferred_element_type=F32)
        for k in range(n):
            o[b + k, c] = acc[:, k * LANES:(k + 1) * LANES].reshape(4, 4, 64, LANES)

    order = (("z", "x"), ("x", "z"))

    def device(ring, k):
        if ring == "z":
            return (t, at(z, k) * 4 + x)
        return (t, z * 4 + at(x, k))

    def rs_send_one(op, b, fl, m, val):
        if m < 6:
            snd, rcv = snd1.at[op, b, fl, m], rcv1.at[op, b, fl, m]
            target = device(order[fl][0], 1 - 2 * (m // 3))
        else:
            snd, rcv = snd2.at[op, b, fl, m - 6], rcv2.at[op, b, fl, m - 6]
            target = device(order[fl][1], m - 5)
        snd[...] = val.astype(BF16)
        copy = pltpu.make_async_remote_copy(
            src_ref=snd, dst_ref=rcv, send_sem=rs_send.at[op, b, fl, m], recv_sem=rs_recv.at[op, b, fl, m],
            device_id=target, device_id_type=MESH)
        begin(("r", op, b, fl, m), copy, copy)

    def own(b, fl, k, half):
        grp = at(pos[order[fl][0]], k)
        if fl == 0:
            return o[b, :, grp, half * 2:half * 2 + 2, 0:32]
        return o[b, :, half * 2:half * 2 + 2, grp, 32:64]

    def rs_first(op, b):
        for d in range(2):
            for fl in range(2):
                rs_send_one(op, b, fl, d * 3, own(b, fl, 2, d))
        for d in range(2):
            for fl in range(2):
                rs_send_one(op, b, fl, d * 3 + 1, own(b, fl, 1 - 2 * d, 1 - d))

    def rs_forward(op, b):
        for d in range(2):
            for fl in range(2):
                arrived(("r", op, b, fl, d * 3))
                rs_send_one(op, b, fl, d * 3 + 2, own(b, fl, 1 - 2 * d, d) + rcv1[op, b, fl, d * 3].astype(F32))

    def rs_middle(op, b):
        for fl in range(2):
            for m in (1, 4, 2, 5):
                arrived(("r", op, b, fl, m))
            for half in range(2):
                q1[b, fl, :, half * 2:half * 2 + 2] = (
                    own(b, fl, 0, half) + rcv1[op, b, fl, 2 - half].astype(F32) + rcv1[op, b, fl, 4 + half].astype(F32)
                )
            for k in (2, 1, 3):
                rs_send_one(op, b, fl, 5 + k, q1[b, fl, :, at(pos[order[fl][1]], k)])

    def rs_end(op, b):
        out = []
        for fl in range(2):
            total = q1[b, fl, :, pos[order[fl][1]]]
            for k in (1, 3, 2):
                arrived(("r", op, b, fl, 5 + k))
                total = total + rcv2[op, b, fl, k - 1].astype(F32)
            out.append(total.reshape(96, LANES))
        return out

    def cols(b):
        return slice(b * LANES, (b + 1) * LANES)

    def get(ref, b):
        return [ref[f, :, cols(b)] for f in range(2)]

    eye = (
        lax.broadcasted_iota(jnp.int32, (256, 256), 0) == lax.broadcasted_iota(jnp.int32, (256, 256), 1)
    ).astype(F32).astype(BF16)

    def turn(j):
        loads[j].wait()
        c2, c = j // 3, j % 3

        def block(i, carry):
            cut = pl.ds(pl.multiple_of(i * 256, 256), 256)
            for kb in range(2):
                tile = stage[j, kb * 256:(kb + 1) * 256, cut]
                turned = lax.dot_general(eye, tile, (((1,), (1,)), ((), ())), preferred_element_type=F32)
                mt[c, cut, c2 * 512 + kb * 256:c2 * 512 + (kb + 1) * 256] = turned.astype(BF16)
            return carry

        lax.fori_loop(0, 4, block, 0)

    def fiber(f):
        return jnp.concatenate([rhs[c, f * 32:(f + 1) * 32, :] for c in range(3)], axis=0)

    def start():
        for load in small:
            load.wait()
        r0 = apply_blocks(fiber(0), fiber(1))
        for f in range(2):
            v1[f] = r0[f]
        parts = [[r0[f][:, cols(b)] for f in range(2)] for b in range(BATCHES)]
        ar_own(0, [inner(part, part) for part in parts])
        for b in range(WIDE):
            g_own(0, b, parts[b])

    def greeted():
        pl.semaphore_wait(barrier, 22)
        ar_start(0)
        for b in range(WIDE):
            g_start(0, b)

    betas, squares = [None] * BATCHES, [None] * BATCHES
    h11, h21, n22 = [None] * BATCHES, [None] * BATCHES, [None] * BATCHES
    kept = {}

    def first_basis():
        tile = ar_end(0)
        for b in range(BATCHES):
            squares[b] = tile[b]
            betas[b] = jnp.sqrt(tile[b] + EPS)

    def basis(b):
        vec = [part / betas[b] for part in get(v1, b)]
        if b >= WIDE:
            g_start(0, b, vec)
        for f in range(2):
            v1[f, :, cols(b)] = vec[f]

    def after_first(b):
        kv = rs_end(0, b)
        vec = get(v1, b)
        wv = apply_blocks(vec[0] + kv[0], vec[1] + kv[1])
        for f in range(2):
            w[f, :, cols(b)] = wv[f]
        g_start(1, b, wv)
        kept[b] = [inner(vec, wv), inner(wv, wv)]
        if b % 2 == 1:
            ar_start(1 + b // 2, kept[b - 1] + kept[b])

    def second_basis(pair):
        tile = ar_end(1 + pair)
        for j in range(2):
            b = pair * 2 + j
            h, ww = tile[j * 2], tile[j * 2 + 1]
            n11 = squares[b] / (squares[b] + EPS)
            left = jnp.maximum(ww - h * h * (2.0 - n11), 0.0)
            h11[b] = h
            h21[b] = jnp.sqrt(left + EPS)
            n22[b] = left / (left + EPS)

    def after_second(b):
        kw = rs_end(1, b)
        first, wv = get(v1, b), get(w, b)
        q = apply_blocks(wv[0] + kw[0], wv[1] + kw[1])
        second = [(wv[f] - h11[b] * first[f]) / h21[b] for f in range(2)]
        zv = [(q[f] - h11[b] * wv[f]) / h21[b] for f in range(2)]
        kept[b] = [inner(first, zv), inner(second, zv), inner(zv, zv)]
        if b % 2 == 1:
            ar_start(3 + b // 2, kept[b - 1] + kept[b])
        for f in range(2):
            w[f, :, cols(b)] = second[f]

    def output(pair):
        tile = ar_end(3 + pair)
        for j in range(2):
            b = pair * 2 + j
            h12, h22, zz = tile[j * 3:j * 3 + 3]
            n11 = squares[b] / (squares[b] + EPS)
            n12 = h11[b] * (1.0 - n11) / h21[b]
            left = zz - h12 * h12 * (2.0 - n11) - h22 * h22 * (2.0 - n22[b]) + 2.0 * h12 * h22 * n12
            h32 = jnp.sqrt(jnp.maximum(left, 0.0) + EPS)
            y1, y2, estimate = least_squares(betas[b], h11[b], h21[b], h12, h22, h32)
            for f in range(2):
                out = y1 * v1[f, :, cols(b)] + y2 * w[f, :, cols(b)]
                for c in range(3):
                    sol[c, f * 32:(f + 1) * 32, cols(b)] = out[c * 32:(c + 1) * 32]
            for i, row in enumerate(((h11[b], h12), (h21[b], h22), (estimate, h32))):
                for k in range(2):
                    arn[i, k:k + 1, cols(b)] = row[k]

    steps = [
        (start,), (greeted,), (turn, 0), (turn, 3), (turn, 6), (turn, 1), (ar_mid, 0), (turn, 4), (turn, 7),
        (turn, 2), (g_forward, 0, 0), (turn, 5), (turn, 8), (first_basis,), (basis, 2), (basis, 3), (multiply, 0, 0, 1, 0),
        (multiply, 0, 0, 1, 1), (g_forward, 0, 1), (multiply, 0, 0, 1, 2), (rs_first, 0, 0), (basis, 0), (basis, 1), (g_forward, 0, 2),
        (multiply, 0, 1, 2, 0), (g_forward, 0, 3), (rs_forward, 0, 0), (multiply, 0, 1, 2, 1),
        (multiply, 0, 1, 2, 2), (rs_first, 0, 1), (rs_first, 0, 2), (rs_middle, 0, 0), (multiply, 0, 3, 1, 0),
        (multiply, 0, 3, 1, 1), (rs_forward, 0, 1), (multiply, 0, 3, 1, 2), (rs_first, 0, 3), (rs_forward, 0, 2),
        (after_first, 0), (rs_middle, 0, 1), (rs_forward, 0, 3), (rs_middle, 0, 2), (g_forward, 1, 0),
        (after_first, 1), (rs_middle, 0, 3), (after_first, 2), (g_forward, 1, 1), (after_first, 3),
        (multiply, 1, 0, 2, 0), (ar_mid, 1), (g_forward, 1, 2), (multiply, 1, 0, 2, 1), (multiply, 1, 0, 2, 2),
        (rs_first, 1, 0), (rs_first, 1, 1), (g_forward, 1, 3), (ar_mid, 2), (second_basis, 0),
        (multiply, 1, 2, 2, 0), (rs_forward, 1, 0), (multiply, 1, 2, 2, 1), (multiply, 1, 2, 2, 2), (rs_first, 1, 2),
        (rs_first, 1, 3), (rs_forward, 1, 1), (rs_middle, 1, 0), (second_basis, 1), (rs_forward, 1, 2),
        (rs_forward, 1, 3), (rs_middle, 1, 1), (after_second, 0), (rs_middle, 1, 2), (rs_middle, 1, 3),
        (after_second, 1), (after_second, 2), (after_second, 3), (ar_mid, 3), (ar_mid, 4), (output, 0), (output, 1),
    ]
    for step, *where in steps:
        step(*where)

    for copy in due.values():
        copy.wait_recv()
    for copy in sent.values():
        copy.wait_send()


def local(mobility, right_side, precond):
    mob = mobility.reshape(9, 512, 1024)
    vmem = pl.BlockSpec(memory_space=pltpu.VMEM)
    dma = pltpu.SemaphoreType.DMA
    n = BATCHES
    return pl.pallas_call(
        kernel,
        out_shape=(jax.ShapeDtypeStruct((3, 64, 512), F32), jax.ShapeDtypeStruct((3, 2, 512), F32)),
        in_specs=[pl.BlockSpec(memory_space=pl.ANY)] * 3,
        out_specs=(vmem, vmem),
        scratch_shapes=[
            pltpu.VMEM((9, 512, 1024), BF16),
            pltpu.VMEM((3, 64, 512), F32),
            pltpu.VMEM((96, 192), F32),
            pltpu.VMEM((3, 1024, 1536), BF16),
            pltpu.VMEM((2, 96, 512), F32),
            pltpu.VMEM((2, 96, 512), F32),
            pltpu.VMEM((n, 3, 4, 4, 64, LANES), F32),
            pltpu.VMEM((n, 2, 3, 4, 32, LANES), F32),
            pltpu.VMEM((2, n, 2, 6, 3, 2, 32, LANES), BF16),
            pltpu.VMEM((2, n, 2, 6, 3, 2, 32, LANES), BF16),
            pltpu.VMEM((2, n, 2, 3, 3, 32, LANES), BF16),
            pltpu.VMEM((2, n, 2, 3, 3, 32, LANES), BF16),
            pltpu.VMEM((WIDE, 3, 8, 64, LANES), F32),
            pltpu.VMEM((2, n, 3, 8, 64, LANES), BF16),
            pltpu.VMEM((5, 8, 8, 128), F32),
            pltpu.VMEM((5, 16, 8, 128), F32),
            dma((9,)),
            dma((2,)),
            dma((2, n, 2, 9)),
            dma((2, n, 2, 9)),
            dma((2, n, 7)),
            dma((2, n, 7)),
            dma((5, 2)),
            dma((5, 2)),
        ],
        compiler_params=pltpu.CompilerParams(
            collective_id=0, has_side_effects=True, vmem_limit_bytes=60 * 1024 * 1024
        ),
    )(mob, right_side, precond)


def solution(mesh):
    return jax.shard_map(
        local,
        mesh=mesh,
        in_specs=(P(None, None, None, "src", None, "tgt"), P(None, ("tgt", "src"), None), P(None, ("tgt", "src"))),
        out_specs=(P(None, ("tgt", "src"), None), P()),
        check_vma=False,
    )
```
